32 devices in a mesh: dp: 2 (over core), row: 4 (over z), col: 4 (over y, x).
Axes of the slice: x: 2, y: 2, z: 4, core: 2. Of those that a mesh axis runs over, the one named last changes fastest.
Arguments:
- tokens: float32 [16384, 2048], P(('dp', 'col'), 'row'), may hold values from -6 to 6
- segments: int32 [8, 2048], P(('dp', 'col')), may hold values from 0 to 15, never falling along the last dimension, each value on 1 to 1024 neighbouring positions
- cotangent: float32 [16384, 2048], P(('dp', 'col'), 'row'), may hold values from -6 to 6
- w_query: bfloat16 [2048, 2048], P('col', 'row'), may hold values from -0.125 to 0.125
- w_key: bfloat16 [2048, 512], P('col', 'row'), may hold values from -0.125 to 0.125
- w_value: bfloat16 [2048, 512], P('col', 'row'), may hold values from -0.125 to 0.125
- w_out: bfloat16 [2048, 2048], P('row', 'col'), may hold values from -1 to 1
- w_gate: bfloat16 [2048, 8192], P('col', 'row'), may hold values from -0.125 to 0.125
- w_up: bfloat16 [2048, 8192], P('col', 'row'), may hold values from -0.125 to 0.125
- w_down: bfloat16 [8192, 2048], P('row', 'col'), may hold values from -0.0625 to 0.0625
- gain_attn: float32 [2048], P('row'), may hold values from 0.5 to 1.5
- gain_mlp: float32 [2048], P('row'), may hold values from 0.5 to 1.5
Outputs:
- hidden_out: float32 [16384, 2048], P(('dp', 'col'), 'row')
- grad_tokens: float32 [16384, 2048], P(('dp', 'col'), 'row')
- grad_w_query: float32 [2048, 2048], P('col', 'row')
- grad_w_key: float32 [2048, 512], P('col', 'row')
- grad_w_value: float32 [2048, 512], P('col', 'row')
- grad_w_out: float32 [2048, 2048], P('row', 'col')
- grad_w_gate: float32 [2048, 8192], P('col', 'row')
- grad_w_up: float32 [2048, 8192], P('col', 'row')
- grad_w_down: float32 [8192, 2048], P('row', 'col')
- grad_gain_attn: float32 [2048], P('row')
- grad_gain_mlp: float32 [2048], P('row')
The draws below stay inside these ranges and needn't reach their ends.
Inputs may be any that keep to these rules, and one draw needn't show every extreme that they name: `segments`: in each row the document numbers never fall; each document has 1 to 1024 tokens, one exactly 1024.
All inputs are finite; a program needn't handle non-finite values.
Results may differ from the reference program's by a relative error of at most 0.013.
Values may be sent and summed in bfloat16 or wider, within the bound.
A program may use at most 384 MiB of HBM per device.

```python
import math
import jax
import jax.numpy as jnp
import numpy as np
from jax import lax

D = 2048
HEADS = 32
KV = 8
HD = 64
FF = 8192
LEN = 2048
QBLOCK = 512
DOC_COUNT = 16
DOC_MOST = 1024
SEQS = 8
TOKENS = 16384


def level_of(rng, dims, cuts, least, largest):
    def one(axis_at, shards_of):
        draws = jax.random.uniform(jax.random.fold_in(jax.random.fold_in(rng, 6), axis_at), (shards_of,), jnp.float32, least / len(cuts), largest / len(cuts))
        return jnp.repeat(jnp.exp(draws), dims[axis_at] // shards_of).reshape((-1,) + (1,) * (len(dims) - axis_at - 1))

    level = one(*cuts[0])
    for cut in cuts[1:]:
        level = level * one(*cut)
    return level


def split_up(count, total, reach, slope):
    loads = [(1 << 20) // math.isqrt(grade ** slope) + 1 for grade in range(2, count + 1)]
    rest, holding = total - reach - (count - 1), [1] * (count - 1)
    while rest > 0:
        movable = [i for i in range(count - 1) if holding[i] < reach]
        pool, left = sum([loads[i] for i in movable]), rest
        for i in movable:
            more = min(reach - holding[i], max(1, left * loads[i] // pool), rest)
            holding[i] = holding[i] + more
            rest = rest - more
    return np.array([reach] + holding)


def ragged(key, count, total, limit, skew):
    if count == 2:
        one = jax.random.randint(key, (), max(1, total - limit), min(limit, total - 1) + 1)
        return jnp.stack([one, total - one])
    sizes = jnp.asarray(split_up(count, total, limit, skew), jnp.int32)
    couples = (count - 1) // 2
    donor, taker = sizes[1:1 + 2 * couples:2], sizes[2:2 + 2 * couples:2]
    margin = jnp.minimum(donor - 1, limit - taker)
    passed = jax.random.randint(jax.random.fold_in(key, 1), (couples,), 0, 1 << 20) % (margin + 1)
    sizes = sizes.at[1:1 + 2 * couples:2].set(donor - passed).at[2:2 + 2 * couples:2].set(taker + passed)
    return sizes[jax.random.permutation(jax.random.fold_in(key, 2), count)]


def normal_values(key, shape, spread, most, pieces=(), kind=jnp.bfloat16):
    level = level_of(key, shape, pieces, -0.22, 0.18) if pieces else 1.0
    result = jax.random.normal(key, shape, jnp.float32) * spread * level
    return jnp.minimum(jnp.maximum(result, -most), most).astype(kind)


def setup_inputs(seed: int = 0) -> dict:
    key_of = jax.random.split(jax.random.key(seed), 13)
    return {
        "tokens": normal_values(key_of[0], (TOKENS, D), 1.0, 6.0, ((0, 8), (1, 4)), jnp.float32),
        "segments": jax.vmap(lambda own: jnp.searchsorted(jnp.cumsum(ragged(own, DOC_COUNT, LEN, DOC_MOST, 2)), jnp.arange(LEN), side="right"))(jax.random.split(key_of[1], SEQS)).reshape((SEQS, LEN)).astype(jnp.int32),
        "cotangent": normal_values(key_of[2], (TOKENS, D), 1.0, 6.0, ((0, 8), (1, 4)), jnp.float32),
        "w_query": normal_values(key_of[3], (D, HEADS * HD), D ** -0.5, 0.125, ((0, 4), (1, 4))),
        "w_key": normal_values(key_of[4], (D, KV * HD), D ** -0.5, 0.125, ((0, 4), (1, 4))),
        "w_value": normal_values(key_of[5], (D, KV * HD), D ** -0.5, 0.125, ((0, 4), (1, 4))),
        "w_out": normal_values(key_of[6], (HEADS * HD, D), (HEADS * HD // 64) ** -0.5, 1.0, ((0, 4), (1, 4))),
        "w_gate": normal_values(key_of[7], (D, FF), D ** -0.5, 0.125, ((0, 4), (1, 4))),
        "w_up": normal_values(key_of[8], (D, FF), D ** -0.5, 0.125, ((0, 4), (1, 4))),
        "w_down": normal_values(key_of[9], (FF, D), FF ** -0.5, 0.0625, ((0, 4), (1, 4))),
        "gain_attn": jnp.clip(1.0 + 0.1 * jax.random.normal(key_of[10], (D,), jnp.float32), 0.5, 1.5),
        "gain_mlp": jnp.clip(1.0 + 0.1 * jax.random.normal(key_of[11], (D,), jnp.float32), 0.5, 1.5),
    }


@jax.custom_vjp
def low(v):
    return lax.optimization_barrier(v.astype(jnp.bfloat16)).astype(jnp.float32)

@jax.custom_vjp
def low_back(v):
    return v

def low_keep(v):
    return (low(v), None)

def low_pass(kept, grad):
    return (grad,)

def back_keep(v):
    return (v, None)

def back_low(kept, grad):
    return (low(grad),)
low.defvjp(low_keep, low_pass)
low_back.defvjp(back_keep, back_low)
NORM_EPS = 1e-05
ROPE_BASE = 500000.0
MASK_FILL = -1e+30
HIGH = lax.Precision.HIGHEST

def matmul(left, right):
    return jnp.dot(left, right, precision=HIGH, preferred_element_type=jnp.float32)

def positions(segment_row):
    token_ids = jnp.arange(segment_row.shape[0], dtype=jnp.int32)
    starts = jnp.concatenate([jnp.ones((1,), dtype=jnp.bool_), segment_row[1:] != segment_row[:-1]])
    doc_start = lax.cummax(jnp.where(starts, token_ids, 0), axis=0)
    return token_ids - doc_start

def rope_tables(places):
    inverse = ROPE_BASE ** (-jnp.arange(HD // 2, dtype=jnp.float32) * 2.0 / HD)
    angles = places.astype(jnp.float32)[:, None] * inverse[None, :]
    return (jnp.cos(angles)[:, None, :], jnp.sin(angles)[:, None, :])

def rotate(values, cosine, sine_part):
    half_width = values.shape[-1] // 2
    first_half = values[..., :half_width]
    second_half = values[..., half_width:]
    return jnp.concatenate([first_half * cosine - second_half * sine_part, second_half * cosine + first_half * sine_part], axis=-1)

def attention(queries, keys_rot, values_low, segment_row):
    blocks = LEN // QBLOCK
    score_scale = 1.0 / math.sqrt(HD)
    token_ids = jnp.arange(LEN, dtype=jnp.int32)
    query_blocks = queries.reshape(blocks, QBLOCK, KV, HEADS // KV, HD)

    def one_block(inputs):
        block_query, block_number = inputs
        block_start = block_number * QBLOCK
        rows_at = block_start + jnp.arange(QBLOCK, dtype=jnp.int32)
        row_segments = lax.dynamic_slice_in_dim(segment_row, block_start, QBLOCK, 0)
        allowed = (rows_at[:, None] >= token_ids[None, :]) & (row_segments[:, None] == segment_row[None, :])
        scores = jnp.einsum('qkgd,tkd->kgqt', block_query, keys_rot, precision=HIGH) * score_scale
        scores = low_back(scores)
        scores = jnp.where(allowed[None, None], scores, MASK_FILL)
        row_max = lax.optimization_barrier(jnp.max(scores, axis=-1, keepdims=True))
        exp_scores = jnp.exp(scores - row_max)
        row_total = lax.optimization_barrier(jnp.sum(exp_scores, axis=-1, keepdims=True))
        probs_low = low(exp_scores / row_total)
        mixed_rows = jnp.einsum('kgqt,tkd->qkgd', probs_low, values_low, precision=HIGH)
        return mixed_rows.reshape(QBLOCK, HEADS * HD)
    outputs = lax.map(jax.checkpoint(one_block), (query_blocks, jnp.arange(blocks, dtype=jnp.int32)))
    return low(low_back(outputs.reshape(LEN, HEADS * HD)))

def block_layer(tokens_in, segment_row, params):
    w_query, w_key, w_value, w_out, w_gate, w_up, w_down, gain_one, gain_two = params
    cosine, sine_part = rope_tables(positions(segment_row))
    scale_one = lax.rsqrt(lax.optimization_barrier(jnp.mean(tokens_in * tokens_in, axis=-1, keepdims=True)) + NORM_EPS)
    normed_one = low(tokens_in * scale_one * gain_one)
    query_raw = low_back(matmul(normed_one, w_query)).reshape(LEN, HEADS, HD)
    key_raw = low_back(matmul(normed_one, w_key)).reshape(LEN, KV, HD)
    values_low = low(low_back(matmul(normed_one, w_value))).reshape(LEN, KV, HD)
    query_rot = low(rotate(query_raw, cosine, sine_part)).reshape(LEN, KV, HEADS // KV, HD)
    key_rot = low(rotate(key_raw, cosine, sine_part))
    mixed = attention(query_rot, key_rot, values_low, segment_row)
    after_attn = tokens_in + low_back(matmul(mixed, w_out))
    scale_two = lax.rsqrt(lax.optimization_barrier(jnp.mean(after_attn * after_attn, axis=-1, keepdims=True)) + NORM_EPS)
    normed_two = low(after_attn * scale_two * gain_two)
    gate_act = low_back(matmul(normed_two, w_gate))
    up_proj = low_back(matmul(normed_two, w_up))
    hidden = low(jax.nn.silu(gate_act) * up_proj)
    return after_attn + low_back(matmul(hidden, w_down))

def reference(tokens, segments, cotangent, w_query, w_key, w_value, w_out, w_gate, w_up, w_down, gain_attn, gain_mlp):
    params = (w_query.astype(jnp.float32), w_key.astype(jnp.float32), w_value.astype(jnp.float32), w_out.astype(jnp.float32), w_gate.astype(jnp.float32), w_up.astype(jnp.float32), w_down.astype(jnp.float32), gain_attn.astype(jnp.float32), gain_mlp.astype(jnp.float32))
    token_seqs = tokens.reshape(SEQS, LEN, D)
    cot_seqs = cotangent.reshape(SEQS, LEN, D)
    zero_grads = jax.tree.map(jnp.zeros_like, params)

    def one_sequence(running, inputs):
        tokens_in, segment_row, cot_row = inputs

        def forward(act_in, weights):
            return block_layer(act_in, segment_row, weights)
        output, pullback = jax.vjp(forward, tokens_in, params)
        grad_in, grad_params = pullback(cot_row)
        return (jax.tree.map(jnp.add, running, grad_params), (output, grad_in))
    totals, (outputs, grads_in) = lax.scan(one_sequence, zero_grads, (token_seqs, segments, cot_seqs))
    return (outputs.reshape(TOKENS, D), grads_in.reshape(TOKENS, D), totals[0], totals[1], totals[2], totals[3], totals[4], totals[5], totals[6], totals[7], totals[8])
```

```python
import functools
import math

import jax
import jax.numpy as jnp
from jax import lax
from jax.experimental import pallas as pl
from jax.experimental.pallas import tpu as pltpu
from jax.sharding import PartitionSpec as P

D = 2048
HEADS = 32
KV = 8
HD = 64
HALF = HD // 2
GROUP = HEADS // KV
BLOCK = 256
ROPE_ROWS = 512

NORM_EPS = 1e-05
ROPE_BASE = 500000.0
MASK_FILL = -1e30
SCORE_SCALE = 1.0 / math.sqrt(HD)
VMEM_BYTES = 40 * 1024 * 1024

NT = (((1,), (1,)), ((), ()))
TN = (((0,), (0,)), ((), ()))
NN = (((1,), (0,)), ((), ()))


def mm(left, right, dims):
    return lax.dot_general(left, right, dims, preferred_element_type=jnp.float32)


def feature_sum(values):
    return lax.psum(values, "row")


def gather_features(values):
    return lax.all_gather(values, "row", axis=1, tiled=True)


def reduce_features(values):
    return lax.psum_scatter(
        values.astype(jnp.bfloat16), "row", scatter_dimension=1, tiled=True
    ).astype(jnp.float32)


def swap_with(values, name, distance):
    pairs = [(i, i ^ distance) for i in range(lax.axis_size(name))]
    return lax.ppermute(values, name, pairs)


def gather_blocks(block, name, axis):
    count, here, size = lax.axis_size(name), lax.axis_index(name), block.shape[axis]
    shape = list(block.shape)
    shape[axis] = size * count
    full = jnp.zeros(shape, block.dtype)
    for distance in range(count):
        piece = swap_with(block, name, distance) if distance else block
        full = lax.dynamic_update_slice_in_dim(full, piece, (here ^ distance) * size, axis)
    return full


def sum_blocks(values, name, axis):
    count, here = lax.axis_size(name), lax.axis_index(name)
    size = values.shape[axis] // count
    total = lax.dynamic_slice_in_dim(values, here * size, size, axis).astype(jnp.float32)
    for distance in range(1, count):
        piece = lax.dynamic_slice_in_dim(values, (here ^ distance) * size, size, axis)
        total = total + swap_with(piece, name, distance).astype(jnp.float32)
    return total.astype(jnp.bfloat16)


def gather_weight(weight, axis):
    return gather_blocks(weight, "col", axis)


def reduce_weight(grad, axis):
    half = sum_blocks(grad.astype(jnp.bfloat16), "dp", 1 - axis)
    part = sum_blocks(half, "col", axis)
    return gather_blocks(part, "dp", 1 - axis).astype(jnp.float32)


def doc_starts(segment_row):
    token_ids = jnp.arange(segment_row.shape[0], dtype=jnp.int32)
    starts = jnp.concatenate([jnp.ones((1,), dtype=jnp.bool_), segment_row[1:] != segment_row[:-1]])
    return lax.cummax(jnp.where(starts, token_ids, 0), axis=0)


def rope_tables(places):
    inverse = ROPE_BASE ** (-jnp.arange(HALF, dtype=jnp.float32) * 2.0 / HD)
    angles = places.astype(jnp.float32)[:, None] * inverse[None, :]
    return (jnp.cos(angles), jnp.sin(angles))


def norm_forward(tokens_in, gain_row):
    totals = feature_sum(jnp.sum(tokens_in * tokens_in, axis=1))
    scale_rows = lax.rsqrt(totals / D + NORM_EPS)[:, None]
    return (scale_rows, (tokens_in * scale_rows * gain_row).astype(jnp.bfloat16))


def norm_backward(tokens_in, scale_rows, gain_row, grad_normed):
    inner_sum = feature_sum(jnp.sum(grad_normed * gain_row * tokens_in, axis=1))[:, None]
    grad_in = scale_rows * gain_row * grad_normed - tokens_in * scale_rows**3 * inner_sum / D
    grad_gain = jnp.sum(grad_normed * tokens_in * scale_rows, axis=0)
    return (grad_in, grad_gain)


def rope_kernel(heads, kv, raw_ref, cos_ref, sin_ref, q_ref, k_ref, v_ref):
    cosine, sine_part = cos_ref[...], sin_ref[...]
    for h in range(heads + kv):
        first = raw_ref[:, h * HD : h * HD + HALF]
        second = raw_ref[:, h * HD + HALF : (h + 1) * HD]
        rot = jnp.concatenate(
            [first * cosine - second * sine_part, second * cosine + first * sine_part], axis=1
        )
        if h < heads:
            q_ref[h] = (rot * SCORE_SCALE).astype(jnp.bfloat16)
        else:
            k_ref[h - heads] = rot.astype(jnp.bfloat16)
    for h in range(kv):
        at = (heads + kv + h) * HD
        v_ref[h] = raw_ref[:, at : at + HD].astype(jnp.bfloat16)


def rope_split(raw, cosine, sine_part, heads, kv):
    rows = raw.shape[0]
    return pl.pallas_call(
        functools.partial(rope_kernel, heads, kv),
        grid=(rows // ROPE_ROWS,),
        in_specs=[
            pl.BlockSpec((ROPE_ROWS, raw.shape[1]), lambda i: (i, 0)),
            pl.BlockSpec((ROPE_ROWS, HALF), lambda i: (i, 0)),
            pl.BlockSpec((ROPE_ROWS, HALF), lambda i: (i, 0)),
        ],
        out_specs=[
            pl.BlockSpec((heads, ROPE_ROWS, HD), lambda i: (0, i, 0)),
            pl.BlockSpec((kv, ROPE_ROWS, HD), lambda i: (0, i, 0)),
            pl.BlockSpec((kv, ROPE_ROWS, HD), lambda i: (0, i, 0)),
        ],
        out_shape=[
            jax.ShapeDtypeStruct((heads, rows, HD), jnp.bfloat16),
            jax.ShapeDtypeStruct((kv, rows, HD), jnp.bfloat16),
            jax.ShapeDtypeStruct((kv, rows, HD), jnp.bfloat16),
        ],
        compiler_params=pltpu.CompilerParams(vmem_limit_bytes=VMEM_BYTES),
        name="rope_split",
    )(raw, cosine, sine_part)


def block_mask(block_at, starts, query_block):
    wide = GROUP * BLOCK
    lane = lax.broadcasted_iota(jnp.int32, (1, wide), 1)
    query_ids = query_block * BLOCK + lax.rem(lane, BLOCK)
    key_ids = block_at * BLOCK + lax.broadcasted_iota(jnp.int32, (BLOCK, wide), 0)
    return (key_ids <= query_ids) & (key_ids >= starts)


def attend_kernel(first_ref, q_ref, k_ref, v_ref, start_ref, o_ref, lse_ref):
    seq, query_block = pl.program_id(0), pl.program_id(2)
    blocks = pl.num_programs(2)
    wide = GROUP * BLOCK
    queries = q_ref[...].reshape(wide, HD)
    starts = jnp.concatenate([start_ref[0]] * GROUP, axis=1)

    def step(at, carry):
        top, total, acc = carry
        rows = pl.ds(pl.multiple_of(at * BLOCK, BLOCK), BLOCK)
        scores = mm(k_ref[0, rows, :], queries, NT)
        scores = jnp.where(block_mask(at, starts, query_block), scores, MASK_FILL)
        new_top = jnp.maximum(top, jnp.max(scores, axis=0, keepdims=True))
        probs = jnp.exp(scores - new_top)
        shrink = jnp.exp(top - new_top)
        total = total * shrink + jnp.sum(probs, axis=0, keepdims=True)
        acc = acc * shrink + mm(v_ref[0, rows, :], probs.astype(jnp.bfloat16), TN)
        return (new_top, total, acc)

    empty = (
        jnp.full((1, wide), MASK_FILL, jnp.float32),
        jnp.zeros((1, wide), jnp.float32),
        jnp.zeros((HD, wide), jnp.float32),
    )
    top, total, acc = lax.fori_loop(
        first_ref[seq * blocks + query_block], query_block + 1, step, empty
    )
    mixed = acc / total
    o_ref[...] = jnp.concatenate(
        [mixed[:, h * BLOCK : (h + 1) * BLOCK].T for h in range(GROUP)], axis=1
    ).astype(jnp.bfloat16)
    lse_ref[0] = top + jnp.log(total)


def attend_forward(first, queries, keys, values, starts, seqs):
    heads, rows, _ = queries.shape
    kv = keys.shape[0]
    length = rows // seqs
    blocks = length // BLOCK
    wide = GROUP * BLOCK
    return pl.pallas_call(
        attend_kernel,
        grid_spec=pltpu.PrefetchScalarGridSpec(
            num_scalar_prefetch=1,
            grid=(seqs, kv, blocks),
            in_specs=[
                pl.BlockSpec((GROUP, BLOCK, HD), lambda s, k, b, f: (k, s * blocks + b, 0)),
                pl.BlockSpec((1, length, HD), lambda s, k, b, f: (k, s, 0)),
                pl.BlockSpec((1, length, HD), lambda s, k, b, f: (k, s, 0)),
                pl.BlockSpec((1, 1, BLOCK), lambda s, k, b, f: (s, 0, b)),
            ],
            out_specs=[
                pl.BlockSpec((BLOCK, GROUP * HD), lambda s, k, b, f: (s * blocks + b, k)),
                pl.BlockSpec((1, 1, wide), lambda s, k, b, f: (k, 0, s * blocks + b)),
            ],
        ),
        out_shape=[
            jax.ShapeDtypeStruct((rows, heads * HD), jnp.bfloat16),
            jax.ShapeDtypeStruct((kv, 1, rows * GROUP), jnp.float32),
        ],
        compiler_params=pltpu.CompilerParams(vmem_limit_bytes=VMEM_BYTES),
        name="attend_forward",
    )(first, queries, keys, values, starts)


def split_heads(block):
    return jnp.concatenate([block[:, h * HD : (h + 1) * HD] for h in range(GROUP)], axis=0)


def grads_kernel(
    first_ref, q_ref, k_ref, v_ref, start_ref, lse_ref, mixed_ref, grad_ref,
    cos_ref, sin_ref, cos_t_ref, sin_t_ref, dq_ref, dk_ref, dv_ref, key_acc, value_acc,
):
    seq, query_block = pl.program_id(0), pl.program_id(2)
    blocks = pl.num_programs(2)
    wide = GROUP * BLOCK

    @pl.when(query_block == 0)
    def _():
        key_acc[...] = jnp.zeros_like(key_acc)
        value_acc[...] = jnp.zeros_like(value_acc)

    queries = q_ref[...].reshape(wide, HD)
    grads = split_heads(grad_ref[...])
    product = grads.astype(jnp.float32) * split_heads(mixed_ref[...]).astype(jnp.float32)
    delta = jnp.sum(product.T, axis=0, keepdims=True)
    log_sums = lse_ref[0]
    starts = jnp.concatenate([start_ref[0]] * GROUP, axis=1)

    def step(at, acc):
        rows = pl.ds(pl.multiple_of(at * BLOCK, BLOCK), BLOCK)
        keys = k_ref[0, rows, :]
        scores = mm(keys, queries, NT)
        scores = jnp.where(block_mask(at, starts, query_block), scores, MASK_FILL)
        probs = jnp.exp(scores - log_sums)
        grad_probs = mm(v_ref[0, rows, :], grads, NT)
        grad_scores = (probs * (grad_probs - delta)).astype(jnp.bfloat16)
        value_acc[rows, :] += mm(probs.astype(jnp.bfloat16), grads, NN)
        key_acc[rows, :] += mm(grad_scores, queries, NN)
        return acc + mm(keys, grad_scores, TN)

    acc = lax.fori_loop(
        first_ref[seq * blocks + query_block],
        query_block + 1,
        step,
        jnp.zeros((HD, wide), jnp.float32),
    )
    cosine, sine_part = cos_t_ref[...], sin_t_ref[...]
    pieces = []
    for h in range(GROUP):
        head = acc[:, h * BLOCK : (h + 1) * BLOCK] * SCORE_SCALE
        top, low = head[:HALF], head[HALF:]
        turned = jnp.concatenate(
            [top * cosine + low * sine_part, low * cosine - top * sine_part], axis=0
        )
        pieces.append(turned.T)
    dq_ref[...] = jnp.concatenate(pieces, axis=1).astype(jnp.bfloat16)

    @pl.when(query_block == blocks - 1)
    def _():
        cosine, sine_part = cos_ref[...], sin_ref[...]
        first, second = key_acc[:, :HALF], key_acc[:, HALF:]
        dk_ref[0] = jnp.concatenate(
            [first * cosine + second * sine_part, second * cosine - first * sine_part], axis=1
        ).astype(jnp.bfloat16)
        dv_ref[0] = value_acc[...].astype(jnp.bfloat16)


def attend_backward(
    first, queries, keys, values, starts, log_sums, mixed, grad_mixed, cosine, sine_part, seqs
):
    heads, rows, _ = queries.shape
    kv = keys.shape[0]
    length = rows // seqs
    blocks = length // BLOCK
    wide = GROUP * BLOCK
    return pl.pallas_call(
        grads_kernel,
        grid_spec=pltpu.PrefetchScalarGridSpec(
            num_scalar_prefetch=1,
            grid=(seqs, kv, blocks),
            in_specs=[
                pl.BlockSpec((GROUP, BLOCK, HD), lambda s, k, b, f: (k, s * blocks + b, 0)),
                pl.BlockSpec((1, length, HD), lambda s, k, b, f: (k, s, 0)),
                pl.BlockSpec((1, length, HD), lambda s, k, b, f: (k, s, 0)),
                pl.BlockSpec((1, 1, BLOCK), lambda s, k, b, f: (s, 0, b)),
                pl.BlockSpec((1, 1, wide), lambda s, k, b, f: (k, 0, s * blocks + b)),
                pl.BlockSpec((BLOCK, GROUP * HD), lambda s, k, b, f: (s * blocks + b, k)),
                pl.BlockSpec((BLOCK, GROUP * HD), lambda s, k, b, f: (s * blocks + b, k)),
                pl.BlockSpec((length, HALF), lambda s, k, b, f: (s, 0)),
                pl.BlockSpec((length, HALF), lambda s, k, b, f: (s, 0)),
                pl.BlockSpec((HALF, BLOCK), lambda s, k, b, f: (0, s * blocks + b)),
                pl.BlockSpec((HALF, BLOCK), lambda s, k, b, f: (0, s * blocks + b)),
            ],
            out_specs=[
                pl.BlockSpec((BLOCK, GROUP * HD), lambda s, k, b, f: (s * blocks + b, k)),
                pl.BlockSpec((1, length, HD), lambda s, k, b, f: (k, s, 0)),
                pl.BlockSpec((1, length, HD), lambda s, k, b, f: (k, s, 0)),
            ],
            scratch_shapes=[
                pltpu.VMEM((length, HD), jnp.float32),
                pltpu.VMEM((length, HD), jnp.float32),
            ],
        ),
        out_shape=[
            jax.ShapeDtypeStruct((rows, heads * HD), jnp.bfloat16),
            jax.ShapeDtypeStruct((kv, rows, HD), jnp.bfloat16),
            jax.ShapeDtypeStruct((kv, rows, HD), jnp.bfloat16),
        ],
        compiler_params=pltpu.CompilerParams(vmem_limit_bytes=VMEM_BYTES),
        name="attend_backward",
    )(
        first, queries, keys, values, starts, log_sums, mixed, grad_mixed,
        cosine, sine_part, cosine.T, sine_part.T,
    )


def per_device(
    tokens,
    segments,
    cotangent,
    w_query,
    w_key,
    w_value,
    w_out,
    w_gate,
    w_up,
    w_down,
    gain_attn,
    gain_mlp,
):
    seqs, length = segments.shape
    rows = tokens.shape[0]
    heads = w_query.shape[1] // HD
    kv = w_key.shape[1] // HD
    wide_q, wide_kv = heads * HD, kv * HD

    qkv_full = gather_weight(jnp.concatenate([w_query, w_key, w_value], axis=1), 0)
    out_full = gather_weight(w_out, 1)
    gate_full = gather_weight(w_gate, 0)
    up_full = gather_weight(w_up, 0)
    down_full = gather_weight(w_down, 1)

    starts = jax.vmap(doc_starts)(segments)
    places = (jnp.arange(length, dtype=jnp.int32)[None, :] - starts).reshape(rows)
    cosine, sine_part = rope_tables(places)
    first = (starts[:, ::BLOCK] // BLOCK).reshape(-1)
    starts = starts[:, None, :]

    scale_one, normed_local = norm_forward(tokens, gain_attn)
    normed_one = gather_features(normed_local)
    normed_one, cotangent_low = lax.optimization_barrier(
        (normed_one, cotangent.astype(jnp.bfloat16))
    )
    grad_branch = gather_features(cotangent_low)
    raw = mm(normed_one, qkv_full, NN)
    queries, keys, values = rope_split(raw, cosine, sine_part, heads, kv)
    mixed, log_sums = attend_forward(first, queries, keys, values, starts, seqs)
    attn_part, grad_branch = lax.optimization_barrier(
        (mm(mixed, out_full, NN).astype(jnp.bfloat16), grad_branch)
    )
    after_attn = tokens + reduce_features(attn_part)
    scale_two, normed_local_two = norm_forward(after_attn, gain_mlp)
    normed_two = gather_features(normed_local_two)
    gate_act = mm(normed_two, gate_full, NN)
    up_proj = mm(normed_two, up_full, NN)
    sigmoid_gate = jax.nn.sigmoid(gate_act)
    hidden = (gate_act * sigmoid_gate * up_proj).astype(jnp.bfloat16)
    result = after_attn + reduce_features(mm(hidden, down_full, NN))

    grad_w_down = reduce_weight(mm(hidden, grad_branch, TN), 1)
    grad_hidden = mm(grad_branch, down_full, NT)
    grad_gate = (
        grad_hidden * up_proj * sigmoid_gate * (1.0 + gate_act * (1.0 - sigmoid_gate))
    ).astype(jnp.bfloat16)
    grad_up = (grad_hidden * gate_act * sigmoid_gate).astype(jnp.bfloat16)
    grad_w_gate = reduce_weight(mm(normed_two, grad_gate, TN), 0)
    grad_w_up = reduce_weight(mm(normed_two, grad_up, TN), 0)
    grad_normed_two = reduce_features(mm(grad_gate, gate_full, NT) + mm(grad_up, up_full, NT))
    grad_after, gain_two = norm_backward(after_attn, scale_two, gain_mlp, grad_normed_two)
    grad_after = cotangent + grad_after
    grad_attn_branch = gather_features(grad_after.astype(jnp.bfloat16))
    grad_w_out = reduce_weight(mm(mixed, grad_attn_branch, TN), 1)
    grad_mixed = mm(grad_attn_branch, out_full, NT).astype(jnp.bfloat16)
    grad_query, grad_key, grad_value = attend_backward(
        first, queries, keys, values, starts, log_sums, mixed, grad_mixed, cosine, sine_part, seqs
    )
    grad_key = jnp.swapaxes(grad_key, 0, 1).reshape(rows, wide_kv)
    grad_value = jnp.swapaxes(grad_value, 0, 1).reshape(rows, wide_kv)
    grad_qkv = jnp.concatenate([grad_query, grad_key, grad_value], axis=1)
    grad_normed_one = reduce_features(mm(grad_qkv, qkv_full, NT))
    grad_w_qkv = reduce_weight(mm(normed_one, grad_qkv, TN), 0)
    grad_before, gain_one = norm_backward(tokens, scale_one, gain_attn, grad_normed_one)
    gains = lax.psum(jnp.stack([gain_one, gain_two]), ("dp", "col"))
    return (
        result,
        grad_after + grad_before,
        grad_w_qkv[:, :wide_q],
        grad_w_qkv[:, wide_q : wide_q + wide_kv],
        grad_w_qkv[:, wide_q + wide_kv :],
        grad_w_out,
        grad_w_gate,
        grad_w_up,
        grad_w_down,
        gains[0],
        gains[1],
    )


def solution(mesh):
    placed = (
        P(("dp", "col"), "row"),
        P(("dp", "col"), None),
        P(("dp", "col"), "row"),
        P("col", "row"),
        P("col", "row"),
        P("col", "row"),
        P("row", "col"),
        P("col", "row"),
        P("col", "row"),
        P("row", "col"),
        P("row"),
        P("row"),
    )
    return jax.shard_map(
        per_device,
        mesh=mesh,
        in_specs=placed,
        out_specs=(
            P(("dp", "col"), "row"),
            P(("dp", "col"), "row"),
            P("col", "row"),
            P("col", "row"),
            P("col", "row"),
            P("row", "col"),
            P("col", "row"),
            P("col", "row"),
            P("row", "col"),
            P("row"),
            P("row"),
        ),
        check_vma=False,
    )
```
